32 devices in a mesh: pair: 8 (over z, x), vir: 4 (over y, core).
Axes of the slice: x: 2, y: 2, z: 4, core: 2. Of those that a mesh axis runs over, the one named last changes fastest.
Arguments:
- amplitudes: float32 [3072, 4096], P(('pair', 'vir')), may hold values from -6 to 6
- integrals: float32 [1536, 1536], P('vir'), may hold values from -0.15625 to 0.15625
- tile_owner: int32 [3072], P(('pair', 'vir')), may hold values from 0 to 7, as said below
- tile_key: int32 [3072], P(('pair', 'vir')), may hold values from 0 to 575
Outputs:
- residual: float32 [3072, 4096], P(('pair', 'vir'))
The draws below stay inside these ranges and needn't reach their ends.
Inputs may be any that keep to these rules, and one draw needn't show every extreme that they name: `tile_owner`: among the 96 tiles of one device no owner is named more than 24 times; one owner, the same for every device, is named exactly 24 times by each device.
All inputs are finite; a program needn't handle non-finite values.
Results may differ from the reference program's by a relative error of at most 0.0003.
Values sent between devices are 32-bit elements; how exact they have to be, the bound alone decides.
A program may use at most 128 MiB of HBM per device.

```python
import jax
import jax.numpy as jnp
from jax import lax

TS = 64
NS = 24
ROWSETS_DEV = 24
TILES_DEV = 96
OWNERS = 8
GROUPS = 4
CAP = 24
TILES = 3072


def draw_tile_owner(key, part):
    device_count = TILES // TILES_DEV
    hottest = jax.random.randint(jax.random.fold_in(key, 11), (), 0, OWNERS)
    position = jnp.arange(TILES_DEV, dtype=jnp.int32)

    def per_device(dev_key):
        offset = jax.random.randint(dev_key, (), 0, OWNERS - 1)
        others = (position - CAP + offset) % (OWNERS - 1)
        others = others + (others >= hottest).astype(jnp.int32)
        owners = jnp.where(position < CAP, hottest, others)
        order = jax.random.permutation(jax.random.fold_in(dev_key, 7), TILES_DEV)
        return owners[order]
    dev_keys = jax.random.split(jax.random.fold_in(key, 23), device_count)
    return jax.vmap(per_device)(dev_keys).reshape(TILES).astype(jnp.int32)


def plant(drawn, rng, least, high):
    spot = [jax.random.randint(jax.random.fold_in(rng, axis), (), 0, length) for axis, length in enumerate(drawn.shape)]
    longest = drawn.shape.index(max(drawn.shape))
    neighbour = spot[:longest] + [(spot[longest] + 1) % drawn.shape[longest]] + spot[longest + 1:]
    return drawn.at[tuple(spot)].set(least).at[tuple(neighbour)].set(high)


def level_of(stream_key, extent, pieces, smallest, largest):
    loudness = 1.0
    for dim, parts in pieces:
        draws = jax.random.uniform(jax.random.fold_in(jax.random.fold_in(stream_key, 6), dim), (parts,), jnp.float32, smallest / len(pieces), largest / len(pieces))
        loudness = loudness * jnp.repeat(jnp.exp(draws), extent[dim] // parts).reshape((-1,) + (1,) * (len(extent) - 1 - dim))
    return loudness


def centred(stream_key, shape, deviation, bound, shards=(), kind=jnp.bfloat16):
    result = jax.random.normal(stream_key, shape, jnp.float32) * deviation
    if len(shards) > 0:
        result = level_of(stream_key, shape, shards, -0.22, 0.18) * result
    return jnp.clip(result, min=-bound, max=bound).astype(kind)


def setup_inputs(seed: int = 0) -> dict:
    key_of = jax.random.split(jax.random.key(seed), 5)
    return {
        "amplitudes": centred(key_of[0], (TILES, TS * TS), 1.0, 6.0, ((0, 32),), jnp.float32),
        "integrals": centred(key_of[1], (NS * TS, NS * TS), (NS * TS) ** -0.5, 0.15625, ((0, 4),), jnp.float32),
        "tile_owner": draw_tile_owner(jax.random.fold_in(key_of[4], 71), 0),
        "tile_key": plant(jax.random.randint(key_of[3], (TILES,), 0, ROWSETS_DEV * NS), jax.random.fold_in(key_of[3], 1), 0, (ROWSETS_DEV * NS) - 1).astype(jnp.int32),
    }


def regroup(values):
    shaped = values.reshape((OWNERS, GROUPS, TILES_DEV) + values.shape[1:])
    shaped = jnp.moveaxis(shaped, 1, 0)
    return shaped.reshape((GROUPS, OWNERS * TILES_DEV) + values.shape[1:])


def reference(amplitudes, integrals, tile_owner, tile_key):
    amp_groups = regroup(amplitudes).reshape(GROUPS, OWNERS * TILES_DEV, TS, TS)
    owner_groups = regroup(tile_owner)
    key_groups = regroup(tile_key)
    column_tables = integrals.reshape(NS * TS, NS, TS)

    def one_group(packed):
        amp_group, owner_group, key_group = packed
        row_block = (owner_group * ROWSETS_DEV + key_group // NS).astype(jnp.int32)
        col_block = (key_group % NS).astype(jnp.int32)
        blocked = jnp.zeros((OWNERS * ROWSETS_DEV, TS, NS, TS), jnp.float32)
        blocked = blocked.at[row_block, :, col_block, :].add(amp_group)
        blocked = blocked.reshape(OWNERS * ROWSETS_DEV, TS, NS * TS)

        def one_batch(batch):
            rows_here, cols_here = batch
            left_rows = blocked[rows_here]
            right_cols = column_tables[:, cols_here, :]
            return jnp.einsum("bik,kbj->bij", left_rows, right_cols, precision=lax.Precision.HIGHEST)

        batches = (row_block.reshape(OWNERS, TILES_DEV), col_block.reshape(OWNERS, TILES_DEV))
        return lax.map(one_batch, batches).reshape(OWNERS * TILES_DEV, TS * TS)

    residual_groups = lax.map(one_group, (amp_groups, owner_groups, key_groups))
    shaped = residual_groups.reshape(GROUPS, OWNERS, TILES_DEV, TS * TS)
    return jnp.moveaxis(shaped, 0, 1).reshape(OWNERS * GROUPS * TILES_DEV, TS * TS)
```

```python
import functools

import jax
import jax.numpy as jnp
from jax import lax
from jax.experimental import pallas as pl
from jax.experimental.pallas import tpu as pltpu
from jax.sharding import PartitionSpec as P

TS = 64
NS = 24
CHUNK = 4
UNROLL = 4
BLOCK = 768
HALF = TS // 2
LANES = 2 * TS


def product_kernel(
    unit_ref, ustart_ref, start_ref, count_ref, home_ref, order_ref, total_ref,
    tiles_ref, high_ref, low_ref, out_ref,
):
    left = lax.broadcasted_iota(jnp.int32, (HALF, LANES), 1) < TS

    @pl.when(pl.program_id(0) == 0)
    def _():
        out_ref[...] = jnp.zeros_like(out_ref)

    def one_unit(u):
        t = unit_ref[0, 0, u]
        base = start_ref[0, 0, t] + CHUNK * (u - ustart_ref[0, 0, t])
        valid = start_ref[0, 0, t] + count_ref[0, 0, t] - base
        column = home_ref[0, t]
        pair_block = column // 2
        tops, bottoms, highs, lows = [], [], [], []
        held = []
        for j in range(CHUNK):
            packed = order_ref[0, 0, base + j]
            p = packed // NS
            s = packed % NS
            tile = jnp.where(j < valid, tiles_ref[p], 0.0)
            held.append((tile, pltpu.roll(tile, TS, 1)))
            rows = pl.ds(pl.multiple_of(s * TS, TS), TS)
            highs.append(high_ref[pair_block, rows, :])
            lows.append(low_ref[pair_block, rows, :])
        for j in range(0, CHUNK, 2):
            (first, first_r), (second, second_r) = held[j], held[j + 1]
            tops.append(jnp.where(left, first, second_r))
            bottoms.append(jnp.where(left, first_r, second))
        lhs = jnp.concatenate(
            [jnp.concatenate(tops, axis=1), jnp.concatenate(bottoms, axis=1)], axis=0
        )
        lhs_high = lhs.astype(jnp.bfloat16)
        lhs_low = (lhs - lhs_high.astype(jnp.float32)).astype(jnp.bfloat16)
        rhs_high = jnp.concatenate(highs, axis=0)
        rhs_low = jnp.concatenate(lows, axis=0)
        both = jnp.dot(
            jnp.concatenate([lhs_high, lhs_low], axis=0), rhs_high,
            preferred_element_type=jnp.float32,
        )
        got = both[:TS] + both[TS:] + jnp.dot(
            lhs_high, rhs_low, preferred_element_type=jnp.float32
        )
        top, bottom = got[:HALF], got[HALF:]
        odd = column % 2 == 1
        rolled = pltpu.roll(jnp.where(odd, top, bottom), TS, 1)
        return t, jnp.where(odd, jnp.where(left, rolled, bottom), jnp.where(left, top, rolled))

    def group(g, carry):
        made = [one_unit(g * UNROLL + i) for i in range(UNROLL)]
        for t, value in made:
            out_ref[t] += value
        return carry

    lax.fori_loop(0, (total_ref[0, 0, 0] + UNROLL - 1) // UNROLL, group, 0)


def product(tiles, ids, mine, high, low, capacity):
    targets = mine.shape[0]
    blocks = ids.shape[0] // BLOCK
    ids = ids.reshape(blocks, BLOCK)
    row = ids // NS
    own_row = mine // NS
    index = jnp.arange(BLOCK, dtype=jnp.int32)
    before = (row[:, :, None] > row[:, None, :]) | (
        (row[:, :, None] == row[:, None, :]) & (index[:, None] > index[None, :])
    )
    position = jnp.sum(before.astype(jnp.int32), axis=2)
    packed = index[None, :] * NS + ids % NS
    order = jnp.sum(
        jnp.where(position[:, None, :] == index[None, :, None], packed[:, None, :], 0), axis=2
    )
    order = jnp.pad(order, ((0, 0), (0, 128)))
    start = jnp.sum((row[:, None, :] < own_row[None, :, None]).astype(jnp.int32), axis=2)
    count = jnp.sum((row[:, None, :] == own_row[None, :, None]).astype(jnp.int32), axis=2)
    units = (count + CHUNK - 1) // CHUNK
    among = jnp.arange(targets, dtype=jnp.int32)
    ustart = jnp.sum(jnp.where(among[None, :, None] > among[None, None, :], units[:, None, :], 0), axis=2)
    total = jnp.sum(units, axis=1)
    most = targets * pl.cdiv(capacity * (BLOCK // targets), CHUNK)
    slot = jnp.arange(most + 128, dtype=jnp.int32)
    uend = ustart + units
    unit = jnp.minimum(
        jnp.sum((uend[:, :, None] <= slot[None, None, :]).astype(jnp.int32), axis=1), targets - 1
    )
    smem = lambda shape: pl.BlockSpec((1, 1) + shape, lambda b: (b, 0, 0), memory_space=pltpu.SMEM)
    whole = lambda shape: pl.BlockSpec(
        shape, lambda b: (0,) * len(shape), memory_space=pltpu.VMEM, pipeline_mode=pl.Buffered(1)
    )
    tables = [unit, ustart, start, count, None, order, total[:, None]]
    specs = [None if v is None else smem((v.shape[1],)) for v in tables]
    tables = [(mine % NS)[None, :] if v is None else v[:, None, :] for v in tables]
    specs[4] = pl.BlockSpec((1, targets), lambda b: (0, 0), memory_space=pltpu.SMEM)
    return pl.pallas_call(
        product_kernel,
        grid=(blocks,),
        out_shape=jax.ShapeDtypeStruct((targets, HALF, LANES), jnp.float32),
        in_specs=specs
        + [
            pl.BlockSpec(
                (BLOCK, HALF, LANES), lambda b: (b, 0, 0),
                pipeline_mode=pl.Buffered(1 if blocks == 1 else 2),
            ),
            whole(high.shape),
            whole(low.shape),
        ],
        out_specs=pl.BlockSpec((targets, HALF, LANES), lambda b: (0, 0, 0)),
        compiler_params=pltpu.CompilerParams(vmem_limit_bytes=(36 if blocks == 1 else 48) * 2**20),
    )(*tables, tiles, high, low)


def per_device(amplitudes, integrals, tile_owner, tile_key):
    targets = amplitudes.shape[0]
    mine = tile_owner * (NS * NS) + tile_key
    ids = lax.all_gather(mine, "pair", axis=0, tiled=True)
    whole = lax.all_gather(integrals, "vir", axis=0, tiled=True)
    tiles = lax.all_gather(
        amplitudes.reshape(targets, HALF, LANES), "pair", axis=0, tiled=True
    )
    whole = whole.reshape(NS * TS, NS // 2, LANES).transpose(1, 0, 2)
    rounded = lax.reduce_precision(whole, 8, 7)
    high = rounded.astype(jnp.bfloat16)
    low = (whole - rounded).astype(jnp.bfloat16)
    capacity = max(2, 2 * targets // lax.axis_size("pair"))
    out = product(tiles, ids, mine, high, low, capacity)
    return out.reshape(targets, TS * TS)


def solution(mesh):
    placed = (P(("pair", "vir"), None), P("vir", None), P(("pair", "vir")), P(("pair", "vir")))
    return jax.shard_map(
        per_device, mesh=mesh, in_specs=placed, out_specs=P(("pair", "vir"), None), check_vma=False
    )
```

```python
import functools

import jax
import jax.numpy as jnp
from jax import lax
from jax.experimental import pallas as pl
from jax.experimental.pallas import tpu as pltpu
from jax.sharding import PartitionSpec as P

TS = 64
NS = 24
CHUNK = 4
UNROLL = 4
BLOCK = 768
HALF = TS // 2
LANES = 2 * TS


def product_kernel(
    unit_ref, ustart_ref, start_ref, count_ref, home_ref, order_ref, total_ref,
    tiles_ref, whole_ref, out_ref, high_ref, low_ref,
):
    left = lax.broadcasted_iota(jnp.int32, (HALF, LANES), 1) < TS

    @pl.when(pl.program_id(0) == 0)
    def _():
        out_ref[...] = jnp.zeros_like(out_ref)

        def split(i, carry):
            rows = pl.ds(pl.multiple_of(i * TS, TS), TS)
            for b in range(NS // 2):
                value = whole_ref[b, rows, :]
                rounded = value.astype(jnp.bfloat16)
                high_ref[b, rows, :] = rounded
                low_ref[b, rows, :] = (value - rounded.astype(jnp.float32)).astype(jnp.bfloat16)
            return carry

        lax.fori_loop(0, NS, split, 0)

    def one_unit(u):
        t = unit_ref[0, 0, u]
        base = start_ref[0, 0, t] + CHUNK * (u - ustart_ref[0, 0, t])
        valid = start_ref[0, 0, t] + count_ref[0, 0, t] - base
        column = home_ref[0, t]
        pair_block = column // 2
        tops, bottoms, highs, lows = [], [], [], []
        held = []
        for j in range(CHUNK):
            packed = order_ref[0, 0, base + j]
            p = packed // NS
            s = packed % NS
            tile = jnp.where(j < valid, tiles_ref[p], 0.0)
            held.append((tile, pltpu.roll(tile, TS, 1)))
            rows = pl.ds(pl.multiple_of(s * TS, TS), TS)
            highs.append(high_ref[pair_block, rows, :])
            lows.append(low_ref[pair_block, rows, :])
        for j in range(0, CHUNK, 2):
            (first, first_r), (second, second_r) = held[j], held[j + 1]
            tops.append(jnp.where(left, first, second_r))
            bottoms.append(jnp.where(left, first_r, second))
        lhs = jnp.concatenate(
            [jnp.concatenate(tops, axis=1), jnp.concatenate(bottoms, axis=1)], axis=0
        )
        lhs_high = lhs.astype(jnp.bfloat16)
        lhs_low = (lhs - lhs_high.astype(jnp.float32)).astype(jnp.bfloat16)
        rhs_high = jnp.concatenate(highs, axis=0)
        rhs_low = jnp.concatenate(lows, axis=0)
        both = jnp.dot(
            jnp.concatenate([lhs_high, lhs_low], axis=0), rhs_high,
            preferred_element_type=jnp.float32,
        )
        got = both[:TS] + both[TS:] + jnp.dot(
            lhs_high, rhs_low, preferred_element_type=jnp.float32
        )
        top, bottom = got[:HALF], got[HALF:]
        odd = column % 2 == 1
        rolled = pltpu.roll(jnp.where(odd, top, bottom), TS, 1)
        return t, jnp.where(odd, jnp.where(left, rolled, bottom), jnp.where(left, top, rolled))

    def group(g, carry):
        made = [one_unit(g * UNROLL + i) for i in range(UNROLL)]
        for t, value in made:
            out_ref[t] += value
        return carry

    lax.fori_loop(0, (total_ref[0, 0, 0] + UNROLL - 1) // UNROLL, group, 0)


def product(tiles, ids, mine, whole, capacity):
    targets = mine.shape[0]
    blocks = ids.shape[0] // BLOCK
    ids = ids.reshape(blocks, BLOCK)
    row = ids // NS
    own_row = mine // NS
    index = jnp.arange(BLOCK, dtype=jnp.int32)
    before = (row[:, :, None] > row[:, None, :]) | (
        (row[:, :, None] == row[:, None, :]) & (index[:, None] > index[None, :])
    )
    position = jnp.sum(before.astype(jnp.int32), axis=2)
    packed = index[None, :] * NS + ids % NS
    order = jnp.sum(
        jnp.where(position[:, None, :] == index[None, :, None], packed[:, None, :], 0), axis=2
    )
    order = jnp.pad(order, ((0, 0), (0, 128)))
    start = jnp.sum((row[:, None, :] < own_row[None, :, None]).astype(jnp.int32), axis=2)
    count = jnp.sum((row[:, None, :] == own_row[None, :, None]).astype(jnp.int32), axis=2)
    units = (count + CHUNK - 1) // CHUNK
    among = jnp.arange(targets, dtype=jnp.int32)
    ustart = jnp.sum(jnp.where(among[None, :, None] > among[None, None, :], units[:, None, :], 0), axis=2)
    total = jnp.sum(units, axis=1)
    most = targets * pl.cdiv(capacity * (BLOCK // targets), CHUNK)
    slot = jnp.arange(most + 128, dtype=jnp.int32)
    uend = ustart + units
    unit = jnp.minimum(
        jnp.sum((uend[:, :, None] <= slot[None, None, :]).astype(jnp.int32), axis=1), targets - 1
    )
    smem = lambda shape: pl.BlockSpec((1, 1) + shape, lambda b: (b, 0, 0), memory_space=pltpu.SMEM)
    tables = [unit, ustart, start, count, None, order, total[:, None]]
    specs = [None if v is None else smem((v.shape[1],)) for v in tables]
    tables = [(mine % NS)[None, :] if v is None else v[:, None, :] for v in tables]
    specs[4] = pl.BlockSpec((1, targets), lambda b: (0, 0), memory_space=pltpu.SMEM)
    return pl.pallas_call(
        product_kernel,
        grid=(blocks,),
        out_shape=jax.ShapeDtypeStruct((targets, HALF, LANES), jnp.float32),
        in_specs=specs
        + [
            pl.BlockSpec(
                (BLOCK, HALF, LANES), lambda b: (b, 0, 0),
                pipeline_mode=pl.Buffered(1 if blocks == 1 else 2),
            ),
            pl.BlockSpec(whole.shape, lambda b: (0, 0, 0), pipeline_mode=pl.Buffered(1)),
        ],
        out_specs=pl.BlockSpec((targets, HALF, LANES), lambda b: (0, 0, 0)),
        scratch_shapes=[pltpu.VMEM(whole.shape, jnp.bfloat16)] * 2,
        compiler_params=pltpu.CompilerParams(vmem_limit_bytes=(40 if blocks == 1 else 54) * 2**20),
    )(*tables, tiles, whole)


MESH = pl.DeviceIdType.MESH
PARTS = 6
LINE = 4
CROSS = PARTS - 1


def gather_kernel(
    tiles_ref, ints_ref, ids_ref, all_ref, whole_ref, allids_ref,
    up_sem, down_sem, over_sem, recv_sem, ids_send, ids_recv, ints_send, ints_recv, local_sem,
):
    pair = lax.axis_index("pair")
    vir = lax.axis_index("vir")
    z, x = pair // 2, pair % 2
    other = pair + 1 - 2 * x
    sibling = vir + 1 - 2 * (vir % 2)
    across = lax.rem(vir + 2, 4)
    depth = ints_ref.shape[1]

    barrier = pltpu.get_barrier_semaphore()
    for k in range(1, 2 * LINE):
        pl.semaphore_signal(
            barrier, inc=1, device_id={"pair": lax.rem(pair + k, 2 * LINE)}, device_id_type=MESH
        )
    for peer in (sibling, across):
        pl.semaphore_signal(barrier, inc=1, device_id={"vir": peer}, device_id_type=MESH)
    pl.semaphore_wait(barrier, 2 * LINE + 1)

    def id_copy(k):
        return pltpu.make_async_remote_copy(
            src_ref=ids_ref, dst_ref=allids_ref.at[pair], send_sem=ids_send.at[k - 1],
            recv_sem=ids_recv.at[k - 1], device_id={"pair": lax.rem(pair + k, 2 * LINE)},
            device_id_type=MESH,
        )

    def id_arrival(k):
        source = lax.rem(pair + 2 * LINE - k, 2 * LINE)
        return pltpu.make_async_remote_copy(
            src_ref=ids_ref, dst_ref=allids_ref.at[source], send_sem=ids_send.at[k - 1],
            recv_sem=ids_recv.at[k - 1], device_id={"pair": source}, device_id_type=MESH,
        )

    def tile_copy(ref, source, part, sems, peer):
        return pltpu.make_async_remote_copy(
            src_ref=ref, dst_ref=all_ref.at[source, part], send_sem=sems.at[source, part],
            recv_sem=recv_sem.at[source, part], device_id={"pair": peer}, device_id_type=MESH,
        )

    def up(ref, source, part):
        return tile_copy(ref, source, part, up_sem, pair + 2)

    def down(ref, source, part):
        return tile_copy(ref, source, part, down_sem, pair - 2)

    def over(ref, source, part):
        return tile_copy(ref, source, part, over_sem, other)

    def arrive(source, part):
        over(all_ref.at[source, part], source, part).wait_recv()

    def ints_copy(ref, owner, index, peer):
        rows = pl.ds(pl.multiple_of(owner * depth, depth), depth)
        return pltpu.make_async_remote_copy(
            src_ref=ref, dst_ref=whole_ref.at[:, rows, :], send_sem=ints_send.at[index],
            recv_sem=ints_recv.at[index], device_id={"vir": peer}, device_id_type=MESH,
        )

    def rows_of(owner):
        return whole_ref.at[:, pl.ds(pl.multiple_of(owner * depth, depth), depth), :]

    for k in range(1, 2 * LINE):
        id_copy(k).start()

    over(tiles_ref.at[CROSS], pair, CROSS).start()

    def own(part, carry):
        @pl.when(z < LINE - 1)
        def _():
            up(tiles_ref.at[part], pair, part).start()

        @pl.when(z > 0)
        def _():
            down(tiles_ref.at[part], pair, part).start()

        @pl.when(part < CROSS)
        def _():
            over(tiles_ref.at[part], pair, part).start()

        return carry

    lax.fori_loop(0, PARTS, own, 0)
    ints_copy(ints_ref, vir, 0, across).start()
    ints_copy(ints_ref, vir, 1, sibling).start()
    locals_ = [
        pltpu.make_async_copy(tiles_ref, all_ref.at[pair], local_sem.at[0]),
        pltpu.make_async_copy(ints_ref, rows_of(vir), local_sem.at[1]),
        pltpu.make_async_copy(ids_ref, allids_ref.at[pair], local_sem.at[2]),
    ]
    for copy in locals_:
        copy.start()

    def from_below(distance, column, part, crosses):
        source = (z - distance) * 2 + column

        @pl.when(z >= distance)
        def _():
            arrive(source, part)

            @pl.when(z < LINE - 1)
            def _():
                up(all_ref.at[source, part], source, part).start()

            if crosses:
                over(all_ref.at[source, part], source, part).start()

    def from_above(distance, column, part, crosses):
        source = (z + distance) * 2 + column

        @pl.when(z + distance < LINE)
        def _():
            arrive(source, part)

            @pl.when(z > 0)
            def _():
                down(all_ref.at[source, part], source, part).start()

            if crosses:
                over(all_ref.at[source, part], source, part).start()

    for distance in range(1, LINE):

        def step(part, carry, distance=distance):
            from_below(distance, x, part, True)
            from_above(distance, x, part, True)
            return carry

        lax.fori_loop(0, CROSS, step, 0)
        from_below(distance, x, CROSS, False)
        from_above(distance, x, CROSS, False)
        if distance == 1:
            arrive(other, CROSS)

            @pl.when(z < LINE - 1)
            def _():
                up(all_ref.at[other, CROSS], other, CROSS).start()

            @pl.when(z > 0)
            def _():
                down(all_ref.at[other, CROSS], other, CROSS).start()

        else:
            from_below(distance - 1, 1 - x, CROSS, False)
            from_above(distance - 1, 1 - x, CROSS, False)
        if distance == 2:
            ints_copy(rows_of(across), across, 0, across).wait_recv()
            ints_copy(rows_of(across), across, 2, sibling).start()
    from_below(LINE - 1, 1 - x, CROSS, False)
    from_above(LINE - 1, 1 - x, CROSS, False)

    def last(part, carry):
        for k in range(LINE):
            arrive(k * 2 + 1 - x, part)
        return carry

    lax.fori_loop(0, CROSS, last, 0)
    ints_copy(rows_of(sibling), sibling, 1, sibling).wait_recv()
    far = lax.rem(sibling + 2, 4)
    ints_copy(rows_of(far), far, 2, sibling).wait_recv()
    for k in range(1, 2 * LINE):
        id_arrival(k).wait_recv()
    for copy in locals_:
        copy.wait()

    def sent(part, carry):
        for k in range(LINE):
            source = k * 2 + x

            @pl.when((k <= z) & (z < LINE - 1))
            def _():
                up(all_ref.at[source, part], source, part).wait_send()

            @pl.when((k >= z) & (z > 0))
            def _():
                down(all_ref.at[source, part], source, part).wait_send()

            @pl.when((part < CROSS) | (k == z))
            def _():
                over(all_ref.at[source, part], source, part).wait_send()

        return carry

    lax.fori_loop(0, PARTS, sent, 0)
    for k in range(LINE):
        source = k * 2 + 1 - x

        @pl.when((k <= z) & (z < LINE - 1))
        def _():
            up(all_ref.at[source, CROSS], source, CROSS).wait_send()

        @pl.when((k >= z) & (z > 0))
        def _():
            down(all_ref.at[source, CROSS], source, CROSS).wait_send()

    for k in range(1, 2 * LINE):
        id_copy(k).wait_send()
    for index in range(3):
        ints_copy(ints_ref, vir, index, sibling).wait_send()


def gathered(tiles, integrals, ids):
    targets, blocks = tiles.shape[0], integrals.shape[0]
    anywhere = pl.BlockSpec(memory_space=pl.ANY)
    slots = (2 * LINE, PARTS)
    dma = pltpu.SemaphoreType.DMA
    all_tiles, whole, all_ids = pl.pallas_call(
        gather_kernel,
        out_shape=[
            jax.ShapeDtypeStruct(slots + (targets // PARTS, HALF, LANES), jnp.float32),
            jax.ShapeDtypeStruct((blocks, 4 * integrals.shape[1], LANES), jnp.float32),
            jax.ShapeDtypeStruct((2 * LINE, 8, LANES), jnp.int32),
        ],
        in_specs=[anywhere] * 3,
        out_specs=[anywhere] * 3,
        scratch_shapes=[dma(slots)] * 4 + [dma((2 * LINE - 1,))] * 2 + [dma((3,))] * 3,
        compiler_params=pltpu.CompilerParams(collective_id=0, has_side_effects=True),
    )(
        tiles.reshape(PARTS, targets // PARTS, HALF, LANES),
        integrals,
        jnp.broadcast_to(jnp.pad(ids, (0, LANES - targets))[None, :], (8, LANES)),
    )
    return all_tiles.reshape(-1, HALF, LANES), whole, all_ids[:, 0, :targets].reshape(-1)


def per_device(amplitudes, integrals, tile_owner, tile_key):
    targets = amplitudes.shape[0]
    pairs = lax.axis_size("pair")
    mine = tile_owner * (NS * NS) + tile_key
    tiles = amplitudes.reshape(targets, HALF, LANES)
    blocked = integrals.reshape(-1, NS // 2, LANES).transpose(1, 0, 2)
    if pairs == 2 * LINE and lax.axis_size("vir") == 4 and targets % PARTS == 0:
        tiles, whole, ids = gathered(tiles, blocked, mine)
    else:
        ids = lax.all_gather(mine, "pair", axis=0, tiled=True)
        whole = lax.all_gather(blocked, "vir", axis=1, tiled=True)
        tiles = lax.all_gather(tiles, "pair", axis=0, tiled=True)
    capacity = max(2, 2 * targets // pairs)
    out = product(tiles, ids, mine, whole, capacity)
    return out.reshape(targets, TS * TS)


def solution(mesh):
    placed = (P(("pair", "vir"), None), P("vir", None), P(("pair", "vir")), P(("pair", "vir")))
    return jax.shard_map(
        per_device, mesh=mesh, in_specs=placed, out_specs=P(("pair", "vir"), None), check_vma=False
    )
```

```python
import functools

import jax
import jax.numpy as jnp
from jax import lax
from jax.experimental import pallas as pl
from jax.experimental.pallas import tpu as pltpu
from jax.sharding import PartitionSpec as P

TS = 64
NS = 24
CHUNK = 4
UNROLL = 4
BLOCK = 768
SCOPED = 16 * 2**20
HALF = TS // 2
LANES = 2 * TS
USTART, START, END, HOME, TOTAL, UNIT = 8, 9, 10, 11, 12, 16


def product_kernel(table_ref, tiles_ref, high_ref, low_ref, out_ref):
    left = lax.broadcasted_iota(jnp.int32, (HALF, LANES), 1) < TS

    @pl.when(pl.program_id(0) == 0)
    def _():
        out_ref[...] = jnp.zeros_like(out_ref)

    def one_unit(u):
        t = table_ref[0, UNIT + u // LANES, u % LANES]
        base = table_ref[0, START, t] + CHUNK * (u - table_ref[0, USTART, t])
        valid = table_ref[0, END, t] - base
        column = table_ref[0, HOME, t]
        pair_block = column // 2
        tops, bottoms, highs, lows = [], [], [], []
        held = []
        for j in range(CHUNK):
            packed = table_ref[0, (base + j) // LANES, (base + j) % LANES]
            p = packed // NS
            s = packed % NS
            tile = jnp.where(j < valid, tiles_ref[p], 0.0)
            held.append((tile, pltpu.roll(tile, TS, 1)))
            rows = pl.ds(pl.multiple_of(s * TS, TS), TS)
            highs.append(high_ref[pair_block, rows, :])
            lows.append(low_ref[pair_block, rows, :])
        for j in range(0, CHUNK, 2):
            (first, first_r), (second, second_r) = held[j], held[j + 1]
            tops.append(jnp.where(left, first, second_r))
            bottoms.append(jnp.where(left, first_r, second))
        lhs = jnp.concatenate(
            [jnp.concatenate(tops, axis=1), jnp.concatenate(bottoms, axis=1)], axis=0
        )
        lhs_high = lhs.astype(jnp.bfloat16)
        lhs_low = (lhs - lhs_high.astype(jnp.float32)).astype(jnp.bfloat16)
        rhs_high = jnp.concatenate(highs, axis=0)
        rhs_low = jnp.concatenate(lows, axis=0)
        both = jnp.dot(
            jnp.concatenate([lhs_high, lhs_low], axis=0), rhs_high,
            preferred_element_type=jnp.float32,
        )
        got = both[:TS] + both[TS:] + jnp.dot(
            lhs_high, rhs_low, preferred_element_type=jnp.float32
        )
        top, bottom = got[:HALF], got[HALF:]
        odd = column % 2 == 1
        rolled = pltpu.roll(jnp.where(odd, top, bottom), TS, 1)
        return t, jnp.where(odd, jnp.where(left, rolled, bottom), jnp.where(left, top, rolled))

    def group(g, carry):
        made = [one_unit(g * UNROLL + i) for i in range(UNROLL)]
        for t, value in made:
            out_ref[t] += value
        return carry

    lax.fori_loop(0, (table_ref[0, TOTAL, 0] + UNROLL - 1) // UNROLL, group, 0)


def unit_rows(targets, capacity):
    return pl.cdiv(targets * pl.cdiv(capacity * (BLOCK // targets), CHUNK) + UNROLL, 8 * LANES) * 8


def tables(ids, mine, capacity):
    targets = mine.shape[0]
    blocks = ids.shape[0] // BLOCK
    ids = ids.reshape(blocks, BLOCK)
    row = ids // NS
    own_row = mine // NS
    index = jnp.arange(BLOCK, dtype=jnp.int32)
    key = row * BLOCK + index[None, :]
    position = jnp.sum((key[:, :, None] > key[:, None, :]).astype(jnp.int32), axis=2)
    packed = index[None, :] * NS + ids % NS
    slot = jnp.arange(8 * LANES, dtype=jnp.int32)
    order = jnp.sum(
        jnp.where(position[:, None, :] == slot[None, :, None], packed[:, None, :], 0), axis=2
    )
    start = jnp.sum((row[:, None, :] < own_row[None, :, None]).astype(jnp.int32), axis=2)
    end = jnp.sum((row[:, None, :] <= own_row[None, :, None]).astype(jnp.int32), axis=2)
    units = (end - start + CHUNK - 1) // CHUNK
    among = jnp.arange(targets, dtype=jnp.int32)
    ustart = jnp.sum(jnp.where(among[None, :, None] > among[None, None, :], units[:, None, :], 0), axis=2)
    slot = jnp.arange(unit_rows(targets, capacity) * LANES, dtype=jnp.int32)
    unit = jnp.minimum(
        jnp.sum(((ustart + units)[:, :, None] <= slot[None, None, :]).astype(jnp.int32), axis=1),
        targets - 1,
    )
    home = jnp.broadcast_to((mine % NS)[None, :], start.shape)
    total = jnp.broadcast_to(jnp.sum(units, axis=1)[:, None], start.shape)
    figures = jnp.stack([ustart, start, end, home, total], axis=1)
    figures = jnp.pad(figures, ((0, 0), (0, UNIT - USTART - 5), (0, LANES - targets)))
    return jnp.concatenate(
        [order.reshape(blocks, 8, LANES), figures, unit.reshape(blocks, -1, LANES)], axis=1
    )


def product(tiles, table, high, low, targets):
    blocks = table.shape[0]
    inside = pl.BlockSpec(memory_space=pltpu.VMEM)
    return pl.pallas_call(
        product_kernel,
        grid=(blocks,),
        out_shape=jax.ShapeDtypeStruct((targets, HALF, LANES), jnp.float32),
        in_specs=[
            pl.BlockSpec((1,) + table.shape[1:], lambda b: (b, 0, 0), memory_space=pltpu.SMEM),
            inside if blocks == 1 else pl.BlockSpec((BLOCK, HALF, LANES), lambda b: (b, 0, 0)),
            inside,
            inside,
        ],
        out_specs=pl.BlockSpec((targets, HALF, LANES), lambda b: (0, 0, 0)),
        compiler_params=pltpu.CompilerParams(vmem_limit_bytes=SCOPED if blocks == 1 else 44 * 2**20),
    )(table, tiles, high, low)


MESH = pl.DeviceIdType.MESH
PARTS = 6
LINE = 4
CROSS = PARTS - 1


def gather_kernel(
    targets, tiles_ref, ints_ref, ids_ref, all_ref, high_ref, low_ref, table_ref,
    whole_ref, allids_ref, key_ref, packed_ref, units_ref, keys, packeds, positions, unit_counts,
    up_sem, down_sem, over_sem, recv_sem, ids_send, ids_recv, ints_send, ints_recv, local_sem,
):
    pair = lax.axis_index("pair")
    vir = lax.axis_index("vir")
    z, x = pair // 2, pair % 2
    other = pair + 1 - 2 * x
    sibling = vir + 1 - 2 * (vir % 2)
    across = lax.rem(vir + 2, 4)
    depth = ints_ref.shape[0]

    barrier = pltpu.get_barrier_semaphore()
    for k in range(1, 2 * LINE):
        pl.semaphore_signal(
            barrier, inc=1, device_id={"pair": lax.rem(pair + k, 2 * LINE)}, device_id_type=MESH
        )
    for peer in (sibling, across):
        pl.semaphore_signal(barrier, inc=1, device_id={"vir": peer}, device_id_type=MESH)
    pl.semaphore_wait(barrier, 2 * LINE + 1)

    def id_copy(k):
        return pltpu.make_async_remote_copy(
            src_ref=ids_ref, dst_ref=allids_ref.at[pl.ds(pair, 1), :], send_sem=ids_send.at[k - 1],
            recv_sem=ids_recv.at[k - 1], device_id={"pair": lax.rem(pair + k, 2 * LINE)},
            device_id_type=MESH,
        )

    def id_arrival(k):
        source = lax.rem(pair + 2 * LINE - k, 2 * LINE)
        return pltpu.make_async_remote_copy(
            src_ref=ids_ref, dst_ref=allids_ref.at[pl.ds(source, 1), :], send_sem=ids_send.at[k - 1],
            recv_sem=ids_recv.at[k - 1], device_id={"pair": source}, device_id_type=MESH,
        )

    def tile_copy(ref, source, part, sems, peer):
        return pltpu.make_async_remote_copy(
            src_ref=ref, dst_ref=all_ref.at[source, part], send_sem=sems.at[source, part],
            recv_sem=recv_sem.at[source, part], device_id={"pair": peer}, device_id_type=MESH,
        )

    def up(ref, source, part):
        return tile_copy(ref, source, part, up_sem, pair + 2)

    def down(ref, source, part):
        return tile_copy(ref, source, part, down_sem, pair - 2)

    def over(ref, source, part):
        return tile_copy(ref, source, part, over_sem, other)

    def arrive(source, part):
        over(all_ref.at[source, part], source, part).wait_recv()

    def ints_copy(ref, owner, index, peer):
        rows = pl.ds(pl.multiple_of(owner * depth, depth), depth)
        return pltpu.make_async_remote_copy(
            src_ref=ref, dst_ref=whole_ref.at[:, rows, :], send_sem=ints_send.at[index],
            recv_sem=ints_recv.at[index], device_id={"vir": peer}, device_id_type=MESH,
        )

    def rows_of(owner):
        return whole_ref.at[:, pl.ds(pl.multiple_of(owner * depth, depth), depth), :]

    for k in range(1, 2 * LINE):
        id_copy(k).start()

    over(tiles_ref.at[CROSS], pair, CROSS).start()

    def own(part, carry):
        @pl.when(z < LINE - 1)
        def _():
            up(tiles_ref.at[part], pair, part).start()

        @pl.when(z > 0)
        def _():
            down(tiles_ref.at[part], pair, part).start()

        @pl.when(part < CROSS)
        def _():
            over(tiles_ref.at[part], pair, part).start()

        return carry

    lax.fori_loop(0, PARTS, own, 0)
    for b in range(NS // 2):
        columns = ints_ref.at[:, pl.ds(b * LANES, LANES)]
        rows = pl.ds(pl.multiple_of(vir * depth, depth), depth)
        pltpu.make_async_copy(columns, whole_ref.at[b, rows, :], local_sem.at[1]).start()
        for index, peer in ((0, across), (1, sibling)):
            pltpu.make_async_remote_copy(
                src_ref=columns, dst_ref=whole_ref.at[b, rows, :], send_sem=ints_send.at[index],
                recv_sem=ints_recv.at[index], device_id={"vir": peer}, device_id_type=MESH,
            ).start()
    locals_ = [
        pltpu.make_async_copy(tiles_ref, all_ref.at[pair], local_sem.at[0]),
        pltpu.make_async_copy(ids_ref, allids_ref.at[pl.ds(pair, 1), :], local_sem.at[2]),
    ]
    for copy in locals_:
        copy.start()
    locals_.pop().wait()
    for k in range(1, 2 * LINE):
        id_arrival(k).wait_recv()

    def to_scalars(source, target):
        copy = pltpu.make_async_copy(source, target, local_sem.at[2])
        copy.start()
        copy.wait()

    def over_tiles(body, initial):
        def device(d, carry):
            return lax.fori_loop(0, targets, lambda i, c: body(d, i, c), carry, unroll=8)

        return lax.fori_loop(0, 2 * LINE, device, initial)

    line = lax.broadcasted_iota(jnp.int32, (8, LANES), 0)
    lane = lax.broadcasted_iota(jnp.int32, (8, LANES), 1)
    slot = line * LANES + lane
    size = 8 * LANES
    ids = allids_ref[...]
    own_key = ids_ref[...] // NS * size
    key = ids // NS * size + slot
    key_ref[...] = key
    packed_ref[...] = (line * targets + lane) * NS + ids % NS
    to_scalars(key_ref, keys)
    to_scalars(packed_ref, packeds)

    def compare(d, i, carry):
        position, start, end = carry
        value = keys[d, i]
        return (
            position + jnp.where(value < key, 1, 0),
            start + jnp.where(value < own_key, 1, 0),
            end + jnp.where(value < own_key + size, 1, 0),
        )

    zero = jnp.zeros((1, LANES), jnp.int32)
    position, start, end = over_tiles(compare, (jnp.zeros_like(key), zero, zero))
    key_ref[...] = position
    units = (end - start + CHUNK - 1) // CHUNK
    units_ref[...] = units
    to_scalars(key_ref, positions)
    to_scalars(units_ref, unit_counts)

    def place(d, i, order):
        return order + jnp.where(slot == positions[d, i], packeds[d, i], 0)

    table_ref[pl.ds(0, 8), :] = over_tiles(place, jnp.zeros_like(key))
    rows = table_ref.shape[0] - UNIT
    place_of = (
        lax.broadcasted_iota(jnp.int32, (rows, LANES), 0) * LANES
        + lax.broadcasted_iota(jnp.int32, (rows, LANES), 1)
    )

    def count(t, carry):
        total, ustart, unit = carry
        ustart = ustart + jnp.where(lane[:1] > t, unit_counts[0, t], 0)
        total = total + unit_counts[0, t]
        return total, ustart, unit + jnp.where(place_of >= total, 1, 0)

    total, ustart, unit = lax.fori_loop(
        0, targets, count, (jnp.int32(0), zero, jnp.zeros((rows, LANES), jnp.int32))
    )
    table_ref[pl.ds(UNIT, rows), :] = jnp.minimum(unit, targets - 1)
    table_ref[pl.ds(USTART, UNIT - USTART), :] = jnp.concatenate(
        [ustart, start, end, ids_ref[...] % NS, zero + total, zero, zero, zero], axis=0
    )

    def from_below(distance, column, part, crosses):
        source = (z - distance) * 2 + column

        @pl.when(z >= distance)
        def _():
            arrive(source, part)

            @pl.when(z < LINE - 1)
            def _():
                up(all_ref.at[source, part], source, part).start()

            if crosses:
                over(all_ref.at[source, part], source, part).start()

    def from_above(distance, column, part, crosses):
        source = (z + distance) * 2 + column

        @pl.when(z + distance < LINE)
        def _():
            arrive(source, part)

            @pl.when(z > 0)
            def _():
                down(all_ref.at[source, part], source, part).start()

            if crosses:
                over(all_ref.at[source, part], source, part).start()

    for distance in range(1, LINE):

        def step(part, carry, distance=distance):
            from_below(distance, x, part, True)
            from_above(distance, x, part, True)
            return carry

        lax.fori_loop(0, CROSS, step, 0)
        from_below(distance, x, CROSS, False)
        from_above(distance, x, CROSS, False)
        if distance == 1:
            arrive(other, CROSS)

            @pl.when(z < LINE - 1)
            def _():
                up(all_ref.at[other, CROSS], other, CROSS).start()

            @pl.when(z > 0)
            def _():
                down(all_ref.at[other, CROSS], other, CROSS).start()

        else:
            from_below(distance - 1, 1 - x, CROSS, False)
            from_above(distance - 1, 1 - x, CROSS, False)
        if distance == 2:
            ints_copy(rows_of(across), across, 0, across).wait_recv()
            ints_copy(rows_of(across), across, 2, sibling).start()
    from_below(LINE - 1, 1 - x, CROSS, False)
    from_above(LINE - 1, 1 - x, CROSS, False)

    ints_copy(rows_of(sibling), sibling, 1, sibling).wait_recv()
    far = lax.rem(sibling + 2, 4)
    ints_copy(rows_of(far), far, 2, sibling).wait_recv()
    pltpu.make_async_copy(rows_of(vir), rows_of(vir), local_sem.at[1]).wait()

    def split(i, carry):
        rows = pl.ds(pl.multiple_of(i * TS, TS), TS)
        for b in range(NS // 2):
            value = whole_ref[b, rows, :]
            rounded = value.astype(jnp.bfloat16)
            high_ref[b, rows, :] = rounded
            low_ref[b, rows, :] = (value - rounded.astype(jnp.float32)).astype(jnp.bfloat16)
        return carry

    lax.fori_loop(0, NS, split, 0)
    def last(part, carry):
        for k in range(LINE):
            arrive(k * 2 + 1 - x, part)
        return carry

    lax.fori_loop(0, CROSS, last, 0)
    for copy in locals_:
        copy.wait()

    def sent(part, carry):
        for k in range(LINE):
            source = k * 2 + x

            @pl.when((k <= z) & (z < LINE - 1))
            def _():
                up(all_ref.at[source, part], source, part).wait_send()

            @pl.when((k >= z) & (z > 0))
            def _():
                down(all_ref.at[source, part], source, part).wait_send()

            @pl.when((part < CROSS) | (k == z))
            def _():
                over(all_ref.at[source, part], source, part).wait_send()

        return carry

    lax.fori_loop(0, PARTS, sent, 0)
    for k in range(LINE):
        source = k * 2 + 1 - x

        @pl.when((k <= z) & (z < LINE - 1))
        def _():
            up(all_ref.at[source, CROSS], source, CROSS).wait_send()

        @pl.when((k >= z) & (z > 0))
        def _():
            down(all_ref.at[source, CROSS], source, CROSS).wait_send()

    for k in range(1, 2 * LINE):
        id_copy(k).wait_send()
    for index in range(3):
        ints_copy(rows_of(vir), vir, index, sibling).wait_send()


def gathered(tiles, integrals, ids, capacity):
    targets = tiles.shape[0]
    shape = (NS // 2, NS * TS, LANES)
    anywhere = pl.BlockSpec(memory_space=pl.ANY)
    inside = pl.BlockSpec(memory_space=pltpu.VMEM)
    slots = (2 * LINE, PARTS)
    dma = pltpu.SemaphoreType.DMA
    all_tiles, high, low, table = pl.pallas_call(
        functools.partial(gather_kernel, targets),
        out_shape=[
            pltpu.VMEM(slots + (targets // PARTS, HALF, LANES), jnp.float32),
            pltpu.VMEM(shape, jnp.bfloat16),
            pltpu.VMEM(shape, jnp.bfloat16),
            jax.ShapeDtypeStruct((UNIT + unit_rows(targets, capacity), LANES), jnp.int32),
        ],
        in_specs=[anywhere, anywhere, inside],
        out_specs=[inside] * 4,
        scratch_shapes=[pltpu.VMEM(shape, jnp.float32)]
        + [pltpu.VMEM((8, LANES), jnp.int32)] * 3
        + [pltpu.VMEM((1, LANES), jnp.int32)]
        + [pltpu.SMEM((8, LANES), jnp.int32)] * 3
        + [pltpu.SMEM((1, LANES), jnp.int32)]
        + [dma(slots)] * 4 + [dma((2 * LINE - 1,))] * 2 + [dma((3,))] * 3,
        compiler_params=pltpu.CompilerParams(
            collective_id=0, has_side_effects=True, vmem_limit_bytes=SCOPED
        ),
    )(
        tiles.reshape(PARTS, targets // PARTS, HALF, LANES),
        integrals,
        jnp.pad(ids, (0, LANES - targets))[None, :],
    )
    return all_tiles.reshape(-1, HALF, LANES), high, low, table[None]


def per_device(amplitudes, integrals, tile_owner, tile_key):
    targets = amplitudes.shape[0]
    pairs = lax.axis_size("pair")
    mine = tile_owner * (NS * NS) + tile_key
    tiles = amplitudes.reshape(targets, HALF, LANES)
    capacity = max(2, 2 * targets // pairs)
    if pairs == 2 * LINE and lax.axis_size("vir") == 4 and targets * pairs == BLOCK and targets % 16 == 0:
        tiles, high, low, table = gathered(tiles, integrals, mine, capacity)
    else:
        ids = lax.all_gather(mine, "pair", axis=0, tiled=True)
        whole = lax.all_gather(integrals, "vir", axis=0, tiled=True)
        whole = whole.reshape(-1, NS // 2, LANES).transpose(1, 0, 2)
        tiles = lax.all_gather(tiles, "pair", axis=0, tiled=True)
        rounded = lax.reduce_precision(whole, 8, 7)
        high = rounded.astype(jnp.bfloat16)
        low = (whole - rounded).astype(jnp.bfloat16)
        table = tables(ids, mine, capacity)
    out = product(tiles, table, high, low, targets)
    return out.reshape(targets, TS * TS)


def solution(mesh):
    placed = (P(("pair", "vir"), None), P("vir", None), P(("pair", "vir")), P(("pair", "vir")))
    return jax.shard_map(
        per_device, mesh=mesh, in_specs=placed, out_specs=P(("pair", "vir"), None), check_vma=False
    )
```

```python
import functools

import jax
import jax.numpy as jnp
from jax import lax
from jax.experimental import pallas as pl
from jax.experimental.pallas import tpu as pltpu
from jax.sharding import PartitionSpec as P

TS = 64
NS = 24
CHUNK = 4
UNROLL = 8
PACK = 32
BLOCK = 768
SCOPED = 16 * 2**20
HALF = TS // 2
LANES = 2 * TS
USTART, START, END, HOME, TOTAL, UNIT = 8, 9, 10, 11, 12, 16


def product_kernel(table_ref, tiles_ref, high_ref, low_ref, out_ref):
    left = lax.broadcasted_iota(jnp.int32, (HALF, LANES), 1) < TS

    @pl.when(pl.program_id(0) == 0)
    def _():
        out_ref[...] = jnp.zeros_like(out_ref)

    def one_unit(u):
        t = table_ref[0, UNIT + (u >> 7), u & (LANES - 1)]
        base = table_ref[0, START, t] + CHUNK * (u - table_ref[0, USTART, t])
        valid = table_ref[0, END, t] - base
        column = table_ref[0, HOME, t]
        pair_block = column >> 1
        tops, bottoms, highs, lows = [], [], [], []
        held = []
        for j in range(CHUNK):
            packed = table_ref[0, (base + j) >> 7, (base + j) & (LANES - 1)]
            p = packed >> 5
            s = packed & (PACK - 1)
            tile = jnp.where(j < valid, tiles_ref[p], 0.0)
            held.append((tile, pltpu.roll(tile, TS, 1)))
            rows = pl.ds(pl.multiple_of(s * TS, TS), TS)
            highs.append(high_ref[pair_block, rows, :])
            lows.append(low_ref[pair_block, rows, :])
        for j in range(0, CHUNK, 2):
            (first, first_r), (second, second_r) = held[j], held[j + 1]
            tops.append(jnp.where(left, first, second_r))
            bottoms.append(jnp.where(left, first_r, second))
        lhs = jnp.concatenate(
            [jnp.concatenate(tops, axis=1), jnp.concatenate(bottoms, axis=1)], axis=0
        )
        lhs_high = lhs.astype(jnp.bfloat16)
        lhs_low = (lhs - lhs_high.astype(jnp.float32)).astype(jnp.bfloat16)
        rhs_high = jnp.concatenate(highs, axis=0)
        rhs_low = jnp.concatenate(lows, axis=0)
        both = jnp.dot(
            jnp.concatenate([lhs_high, lhs_low], axis=0), rhs_high,
            preferred_element_type=jnp.float32,
        )
        got = both[:TS] + both[TS:] + jnp.dot(
            lhs_high, rhs_low, preferred_element_type=jnp.float32
        )
        top, bottom = got[:HALF], got[HALF:]
        odd = (column & 1) == 1
        rolled = pltpu.roll(jnp.where(odd, top, bottom), TS, 1)
        return t, jnp.where(odd, jnp.where(left, rolled, bottom), jnp.where(left, top, rolled))

    def group(g, carry):
        made = [one_unit(g * UNROLL + i) for i in range(UNROLL)]
        for t, value in made:
            out_ref[t] += value
        return carry

    lax.fori_loop(0, (table_ref[0, TOTAL, 0] + UNROLL - 1) // UNROLL, group, 0)


def unit_rows(targets, capacity):
    return pl.cdiv(targets * pl.cdiv(capacity * (BLOCK // targets), CHUNK) + UNROLL, 8 * LANES) * 8


def tables(ids, mine, capacity):
    targets = mine.shape[0]
    blocks = ids.shape[0] // BLOCK
    ids = ids.reshape(blocks, BLOCK)
    row = ids // NS
    own_row = mine // NS
    index = jnp.arange(BLOCK, dtype=jnp.int32)
    key = row * BLOCK + index[None, :]
    position = jnp.sum((key[:, :, None] > key[:, None, :]).astype(jnp.int32), axis=2)
    packed = index[None, :] * PACK + ids % NS
    slot = jnp.arange(8 * LANES, dtype=jnp.int32)
    order = jnp.sum(
        jnp.where(position[:, None, :] == slot[None, :, None], packed[:, None, :], 0), axis=2
    )
    start = jnp.sum((row[:, None, :] < own_row[None, :, None]).astype(jnp.int32), axis=2)
    end = jnp.sum((row[:, None, :] <= own_row[None, :, None]).astype(jnp.int32), axis=2)
    units = (end - start + CHUNK - 1) // CHUNK
    among = jnp.arange(targets, dtype=jnp.int32)
    ustart = jnp.sum(jnp.where(among[None, :, None] > among[None, None, :], units[:, None, :], 0), axis=2)
    slot = jnp.arange(unit_rows(targets, capacity) * LANES, dtype=jnp.int32)
    unit = jnp.minimum(
        jnp.sum(((ustart + units)[:, :, None] <= slot[None, None, :]).astype(jnp.int32), axis=1),
        targets - 1,
    )
    home = jnp.broadcast_to((mine % NS)[None, :], start.shape)
    total = jnp.broadcast_to(jnp.sum(units, axis=1)[:, None], start.shape)
    figures = jnp.stack([ustart, start, end, home, total], axis=1)
    figures = jnp.pad(figures, ((0, 0), (0, UNIT - USTART - 5), (0, LANES - targets)))
    return jnp.concatenate(
        [order.reshape(blocks, 8, LANES), figures, unit.reshape(blocks, -1, LANES)], axis=1
    )


def product(tiles, table, high, low, targets):
    blocks = table.shape[0]
    inside = pl.BlockSpec(memory_space=pltpu.VMEM)
    return pl.pallas_call(
        product_kernel,
        grid=(blocks,),
        out_shape=jax.ShapeDtypeStruct((targets, HALF, LANES), jnp.float32),
        in_specs=[
            pl.BlockSpec((1,) + table.shape[1:], lambda b: (b, 0, 0), memory_space=pltpu.SMEM),
            inside if blocks == 1 else pl.BlockSpec((BLOCK, HALF, LANES), lambda b: (b, 0, 0)),
            inside,
            inside,
        ],
        out_specs=pl.BlockSpec((targets, HALF, LANES), lambda b: (0, 0, 0)),
        compiler_params=pltpu.CompilerParams(vmem_limit_bytes=SCOPED if blocks == 1 else 44 * 2**20),
    )(table, tiles, high, low)


MESH = pl.DeviceIdType.MESH
PARTS = 12
LINE = 4
CROSS = PARTS - 2


def gather_kernel(
    targets, tiles_ref, ints_ref, ids_ref, all_ref, high_ref, low_ref, table_ref,
    whole_ref, allids_ref, key_ref, packed_ref, units_ref, keys, packeds, positions, unit_counts,
    up_sem, down_sem, over_sem, recv_sem, ids_send, ids_recv, ints_send, ints_recv, local_sem,
):
    pair = lax.axis_index("pair")
    vir = lax.axis_index("vir")
    z, x = pair // 2, pair % 2
    other = pair + 1 - 2 * x
    sibling = vir + 1 - 2 * (vir % 2)
    across = lax.rem(vir + 2, 4)
    depth = ints_ref.shape[0]

    barrier = pltpu.get_barrier_semaphore()
    for k in range(1, 2 * LINE):
        pl.semaphore_signal(
            barrier, inc=1, device_id={"pair": lax.rem(pair + k, 2 * LINE)}, device_id_type=MESH
        )
    for peer in (sibling, across):
        pl.semaphore_signal(barrier, inc=1, device_id={"vir": peer}, device_id_type=MESH)
    pl.semaphore_wait(barrier, 2 * LINE + 1)

    def id_copy(k):
        return pltpu.make_async_remote_copy(
            src_ref=ids_ref, dst_ref=allids_ref.at[pl.ds(pair, 1), :], send_sem=ids_send.at[k - 1],
            recv_sem=ids_recv.at[k - 1], device_id={"pair": lax.rem(pair + k, 2 * LINE)},
            device_id_type=MESH,
        )

    def id_arrival(k):
        source = lax.rem(pair + 2 * LINE - k, 2 * LINE)
        return pltpu.make_async_remote_copy(
            src_ref=ids_ref, dst_ref=allids_ref.at[pl.ds(source, 1), :], send_sem=ids_send.at[k - 1],
            recv_sem=ids_recv.at[k - 1], device_id={"pair": source}, device_id_type=MESH,
        )

    def tile_copy(ref, source, part, sems, peer):
        return pltpu.make_async_remote_copy(
            src_ref=ref, dst_ref=all_ref.at[source, part], send_sem=sems.at[source, part],
            recv_sem=recv_sem.at[source, part], device_id={"pair": peer}, device_id_type=MESH,
        )

    def up(ref, source, part):
        return tile_copy(ref, source, part, up_sem, pair + 2)

    def down(ref, source, part):
        return tile_copy(ref, source, part, down_sem, pair - 2)

    def over(ref, source, part):
        return tile_copy(ref, source, part, over_sem, other)

    def arrive(source, part):
        over(all_ref.at[source, part], source, part).wait_recv()

    def ints_copy(ref, owner, index, peer):
        rows = pl.ds(pl.multiple_of(owner * depth, depth), depth)
        return pltpu.make_async_remote_copy(
            src_ref=ref, dst_ref=whole_ref.at[:, rows, :], send_sem=ints_send.at[index],
            recv_sem=ints_recv.at[index], device_id={"vir": peer}, device_id_type=MESH,
        )

    def rows_of(owner):
        return whole_ref.at[:, pl.ds(pl.multiple_of(owner * depth, depth), depth), :]

    for k in range(1, 2 * LINE):
        id_copy(k).start()

    for part in range(CROSS, PARTS):
        over(tiles_ref.at[part], pair, part).start()

    def own(part, carry):
        @pl.when(z < LINE - 1)
        def _():
            up(tiles_ref.at[part], pair, part).start()

        @pl.when(z > 0)
        def _():
            down(tiles_ref.at[part], pair, part).start()

        @pl.when(part < CROSS)
        def _():
            over(tiles_ref.at[part], pair, part).start()

        return carry

    lax.fori_loop(0, PARTS, own, 0)
    for b in range(NS // 2):
        columns = ints_ref.at[:, pl.ds(b * LANES, LANES)]
        rows = pl.ds(pl.multiple_of(vir * depth, depth), depth)
        pltpu.make_async_copy(columns, whole_ref.at[b, rows, :], local_sem.at[1]).start()
        for index, peer in ((0, across), (1, sibling)):
            pltpu.make_async_remote_copy(
                src_ref=columns, dst_ref=whole_ref.at[b, rows, :], send_sem=ints_send.at[index],
                recv_sem=ints_recv.at[index], device_id={"vir": peer}, device_id_type=MESH,
            ).start()
    locals_ = [
        pltpu.make_async_copy(tiles_ref, all_ref.at[pair], local_sem.at[0]),
        pltpu.make_async_copy(ids_ref, allids_ref.at[pl.ds(pair, 1), :], local_sem.at[2]),
    ]
    for copy in locals_:
        copy.start()
    locals_.pop().wait()
    for k in range(1, 2 * LINE):
        id_arrival(k).wait_recv()

    def to_scalars(source, target):
        copy = pltpu.make_async_copy(source, target, local_sem.at[2])
        copy.start()
        copy.wait()

    def over_tiles(body, initial):
        def device(d, carry):
            return lax.fori_loop(0, targets, lambda i, c: body(d, i, c), carry, unroll=8)

        return lax.fori_loop(0, 2 * LINE, device, initial)

    line = lax.broadcasted_iota(jnp.int32, (8, LANES), 0)
    lane = lax.broadcasted_iota(jnp.int32, (8, LANES), 1)
    slot = line * LANES + lane
    size = 8 * LANES
    ids = allids_ref[...]
    own_key = ids_ref[...] // NS * size
    key = ids // NS * size + slot
    key_ref[...] = key
    packed_ref[...] = (line * targets + lane) * PACK + ids % NS
    to_scalars(key_ref, keys)
    to_scalars(packed_ref, packeds)

    def compare(d, i, carry):
        position, start, end = carry
        value = keys[d, i]
        return (
            position + jnp.where(value < key, 1, 0),
            start + jnp.where(value < own_key, 1, 0),
            end + jnp.where(value < own_key + size, 1, 0),
        )

    zero = jnp.zeros((1, LANES), jnp.int32)
    position, start, end = over_tiles(compare, (jnp.zeros_like(key), zero, zero))
    key_ref[...] = position
    units = (end - start + CHUNK - 1) // CHUNK
    units_ref[...] = units
    to_scalars(key_ref, positions)
    to_scalars(units_ref, unit_counts)

    def place(d, i, order):
        return order + jnp.where(slot == positions[d, i], packeds[d, i], 0)

    table_ref[pl.ds(0, 8), :] = over_tiles(place, jnp.zeros_like(key))
    rows = table_ref.shape[0] - UNIT
    place_of = (
        lax.broadcasted_iota(jnp.int32, (rows, LANES), 0) * LANES
        + lax.broadcasted_iota(jnp.int32, (rows, LANES), 1)
    )

    def count(t, carry):
        total, ustart, unit = carry
        ustart = ustart + jnp.where(lane[:1] > t, unit_counts[0, t], 0)
        total = total + unit_counts[0, t]
        return total, ustart, unit + jnp.where(place_of >= total, 1, 0)

    total, ustart, unit = lax.fori_loop(
        0, targets, count, (jnp.int32(0), zero, jnp.zeros((rows, LANES), jnp.int32))
    )
    table_ref[pl.ds(UNIT, rows), :] = jnp.minimum(unit, targets - 1)
    table_ref[pl.ds(USTART, UNIT - USTART), :] = jnp.concatenate(
        [ustart, start, end, ids_ref[...] % NS, zero + total, zero, zero, zero], axis=0
    )

    def from_below(distance, column, part, crosses):
        source = (z - distance) * 2 + column

        @pl.when(z >= distance)
        def _():
            arrive(source, part)

            @pl.when(z < LINE - 1)
            def _():
                up(all_ref.at[source, part], source, part).start()

            if crosses:
                over(all_ref.at[source, part], source, part).start()

    def from_above(distance, column, part, crosses):
        source = (z + distance) * 2 + column

        @pl.when(z + distance < LINE)
        def _():
            arrive(source, part)

            @pl.when(z > 0)
            def _():
                down(all_ref.at[source, part], source, part).start()

            if crosses:
                over(all_ref.at[source, part], source, part).start()

    for distance in range(1, LINE):

        def step(part, carry, distance=distance):
            from_below(distance, x, part, True)
            from_above(distance, x, part, True)
            return carry

        lax.fori_loop(0, CROSS, step, 0)

        def own_column(part, carry, distance=distance):
            from_below(distance, x, part, False)
            from_above(distance, x, part, False)
            return carry

        def other_column(part, carry, distance=distance):
            if distance > 1:
                from_below(distance - 1, 1 - x, part, False)
                from_above(distance - 1, 1 - x, part, False)
                return carry
            arrive(other, part)

            @pl.when(z < LINE - 1)
            def _():
                up(all_ref.at[other, part], other, part).start()

            @pl.when(z > 0)
            def _():
                down(all_ref.at[other, part], other, part).start()

            return carry

        lax.fori_loop(CROSS, PARTS, own_column, 0)
        lax.fori_loop(CROSS, PARTS, other_column, 0)
        if distance == 2:
            ints_copy(rows_of(across), across, 0, across).wait_recv()
            ints_copy(rows_of(across), across, 2, sibling).start()
    for part in range(CROSS, PARTS):
        from_below(LINE - 1, 1 - x, part, False)
        from_above(LINE - 1, 1 - x, part, False)

    ints_copy(rows_of(sibling), sibling, 1, sibling).wait_recv()
    far = lax.rem(sibling + 2, 4)
    ints_copy(rows_of(far), far, 2, sibling).wait_recv()
    pltpu.make_async_copy(rows_of(vir), rows_of(vir), local_sem.at[1]).wait()

    def split(i, carry):
        rows = pl.ds(pl.multiple_of(i * TS, TS), TS)
        for b in range(NS // 2):
            value = whole_ref[b, rows, :]
            rounded = value.astype(jnp.bfloat16)
            high_ref[b, rows, :] = rounded
            low_ref[b, rows, :] = (value - rounded.astype(jnp.float32)).astype(jnp.bfloat16)
        return carry

    lax.fori_loop(0, NS, split, 0)
    def last(part, carry):
        for k in range(LINE):
            arrive(k * 2 + 1 - x, part)
        return carry

    lax.fori_loop(0, CROSS, last, 0)
    for copy in locals_:
        copy.wait()

    def sent(part, carry):
        for k in range(LINE):
            source = k * 2 + x

            @pl.when((k <= z) & (z < LINE - 1))
            def _():
                up(all_ref.at[source, part], source, part).wait_send()

            @pl.when((k >= z) & (z > 0))
            def _():
                down(all_ref.at[source, part], source, part).wait_send()

            @pl.when((part < CROSS) | (k == z))
            def _():
                over(all_ref.at[source, part], source, part).wait_send()

        return carry

    lax.fori_loop(0, PARTS, sent, 0)

    def crossed(part, carry):
        for k in range(LINE):
            source = k * 2 + 1 - x

            @pl.when((k <= z) & (z < LINE - 1))
            def _():
                up(all_ref.at[source, part], source, part).wait_send()

            @pl.when((k >= z) & (z > 0))
            def _():
                down(all_ref.at[source, part], source, part).wait_send()

        return carry

    lax.fori_loop(CROSS, PARTS, crossed, 0)
    for k in range(1, 2 * LINE):
        id_copy(k).wait_send()
    for index in range(3):
        ints_copy(rows_of(vir), vir, index, sibling).wait_send()


def gathered(tiles, integrals, ids, capacity):
    targets = tiles.shape[0]
    shape = (NS // 2, NS * TS, LANES)
    anywhere = pl.BlockSpec(memory_space=pl.ANY)
    inside = pl.BlockSpec(memory_space=pltpu.VMEM)
    slots = (2 * LINE, PARTS)
    dma = pltpu.SemaphoreType.DMA
    all_tiles, high, low, table = pl.pallas_call(
        functools.partial(gather_kernel, targets),
        out_shape=[
            pltpu.VMEM(slots + (targets // PARTS, HALF, LANES), jnp.float32),
            pltpu.VMEM(shape, jnp.bfloat16),
            pltpu.VMEM(shape, jnp.bfloat16),
            jax.ShapeDtypeStruct((UNIT + unit_rows(targets, capacity), LANES), jnp.int32),
        ],
        in_specs=[anywhere, anywhere, inside],
        out_specs=[inside] * 4,
        scratch_shapes=[pltpu.VMEM(shape, jnp.float32)]
        + [pltpu.VMEM((8, LANES), jnp.int32)] * 3
        + [pltpu.VMEM((1, LANES), jnp.int32)]
        + [pltpu.SMEM((8, LANES), jnp.int32)] * 3
        + [pltpu.SMEM((1, LANES), jnp.int32)]
        + [dma(slots)] * 4 + [dma((2 * LINE - 1,))] * 2 + [dma((3,))] * 3,
        compiler_params=pltpu.CompilerParams(
            collective_id=0, has_side_effects=True, vmem_limit_bytes=SCOPED
        ),
    )(
        tiles.reshape(PARTS, targets // PARTS, HALF, LANES),
        integrals,
        jnp.pad(ids, (0, LANES - targets))[None, :],
    )
    return all_tiles.reshape(-1, HALF, LANES), high, low, table[None]


def per_device(amplitudes, integrals, tile_owner, tile_key):
    targets = amplitudes.shape[0]
    pairs = lax.axis_size("pair")
    mine = tile_owner * (NS * NS) + tile_key
    tiles = amplitudes.reshape(targets, HALF, LANES)
    capacity = max(2, 2 * targets // pairs)
    if pairs == 2 * LINE and lax.axis_size("vir") == 4 and targets * pairs == BLOCK and targets % PARTS == 0:
        tiles, high, low, table = gathered(tiles, integrals, mine, capacity)
    else:
        ids = lax.all_gather(mine, "pair", axis=0, tiled=True)
        whole = lax.all_gather(integrals, "vir", axis=0, tiled=True)
        whole = whole.reshape(-1, NS // 2, LANES).transpose(1, 0, 2)
        tiles = lax.all_gather(tiles, "pair", axis=0, tiled=True)
        rounded = lax.reduce_precision(whole, 8, 7)
        high = rounded.astype(jnp.bfloat16)
        low = (whole - rounded).astype(jnp.bfloat16)
        table = tables(ids, mine, capacity)
    out = product(tiles, table, high, low, targets)
    return out.reshape(targets, TS * TS)


def solution(mesh):
    placed = (P(("pair", "vir"), None), P("vir", None), P(("pair", "vir")), P(("pair", "vir")))
    return jax.shard_map(
        per_device, mesh=mesh, in_specs=placed, out_specs=P(("pair", "vir"), None), check_vma=False
    )
```

```python
import functools

import jax
import jax.numpy as jnp
from jax import lax
from jax.experimental import pallas as pl
from jax.experimental.pallas import tpu as pltpu
from jax.sharding import PartitionSpec as P

TS = 64
NS = 24
CHUNK = 4
UNROLL = 16
PACK = 32
BLOCK = 768
SCOPED = 16 * 2**20
HALF = TS // 2
LANES = 2 * TS
USTART, START, END, HOME, TOTAL, UNIT = 8, 9, 10, 11, 12, 16


def product_kernel(table_ref, tiles_ref, high_ref, low_ref, out_ref):
    left = lax.broadcasted_iota(jnp.int32, (HALF, LANES), 1) < TS

    @pl.when(pl.program_id(0) == 0)
    def _():
        out_ref[...] = jnp.zeros_like(out_ref)

    def one_unit(u):
        t = table_ref[0, UNIT + (u >> 7), u & (LANES - 1)]
        base = table_ref[0, START, t] + CHUNK * (u - table_ref[0, USTART, t])
        valid = table_ref[0, END, t] - base
        column = table_ref[0, HOME, t]
        pair_block = column >> 1
        tops, bottoms, highs, lows = [], [], [], []
        held = []
        for j in range(CHUNK):
            packed = table_ref[0, (base + j) >> 7, (base + j) & (LANES - 1)]
            p = packed >> 5
            s = packed & (PACK - 1)
            tile = jnp.where(j < valid, tiles_ref[p], 0.0)
            held.append((tile, pltpu.roll(tile, TS, 1)))
            rows = pl.ds(pl.multiple_of(s * TS, TS), TS)
            highs.append(high_ref[pair_block, rows, :])
            lows.append(low_ref[pair_block, rows, :])
        for j in range(0, CHUNK, 2):
            (first, first_r), (second, second_r) = held[j], held[j + 1]
            tops.append(jnp.where(left, first, second_r))
            bottoms.append(jnp.where(left, first_r, second))
        lhs = jnp.concatenate(
            [jnp.concatenate(tops, axis=1), jnp.concatenate(bottoms, axis=1)], axis=0
        )
        lhs_high = lhs.astype(jnp.bfloat16)
        lhs_low = (lhs - lhs_high.astype(jnp.float32)).astype(jnp.bfloat16)
        rhs_high = jnp.concatenate(highs, axis=0)
        rhs_low = jnp.concatenate(lows, axis=0)
        both = jnp.dot(
            jnp.concatenate([lhs_high, lhs_low], axis=0), rhs_high,
            preferred_element_type=jnp.float32,
        )
        got = both[:TS] + both[TS:] + jnp.dot(
            lhs_high, rhs_low, preferred_element_type=jnp.float32
        )
        top, bottom = got[:HALF], got[HALF:]
        odd = (column & 1) == 1
        rolled = pltpu.roll(jnp.where(odd, top, bottom), TS, 1)
        return t, jnp.where(odd, jnp.where(left, rolled, bottom), jnp.where(left, top, rolled))

    def group(g, carry):
        made = [one_unit(g * UNROLL + i) for i in range(UNROLL)]
        for t, value in made:
            out_ref[t] += value
        return carry

    lax.fori_loop(0, (table_ref[0, TOTAL, 0] + UNROLL - 1) // UNROLL, group, 0)


def unit_rows(targets, capacity):
    return pl.cdiv(targets * pl.cdiv(capacity * (BLOCK // targets), CHUNK) + UNROLL, 8 * LANES) * 8


def tables(ids, mine, capacity):
    targets = mine.shape[0]
    blocks = ids.shape[0] // BLOCK
    ids = ids.reshape(blocks, BLOCK)
    row = ids // NS
    own_row = mine // NS
    index = jnp.arange(BLOCK, dtype=jnp.int32)
    key = row * BLOCK + index[None, :]
    position = jnp.sum((key[:, :, None] > key[:, None, :]).astype(jnp.int32), axis=2)
    packed = index[None, :] * PACK + ids % NS
    slot = jnp.arange(8 * LANES, dtype=jnp.int32)
    order = jnp.sum(
        jnp.where(position[:, None, :] == slot[None, :, None], packed[:, None, :], 0), axis=2
    )
    start = jnp.sum((row[:, None, :] < own_row[None, :, None]).astype(jnp.int32), axis=2)
    end = jnp.sum((row[:, None, :] <= own_row[None, :, None]).astype(jnp.int32), axis=2)
    units = (end - start + CHUNK - 1) // CHUNK
    among = jnp.arange(targets, dtype=jnp.int32)
    ustart = jnp.sum(jnp.where(among[None, :, None] > among[None, None, :], units[:, None, :], 0), axis=2)
    slot = jnp.arange(unit_rows(targets, capacity) * LANES, dtype=jnp.int32)
    unit = jnp.minimum(
        jnp.sum(((ustart + units)[:, :, None] <= slot[None, None, :]).astype(jnp.int32), axis=1),
        targets - 1,
    )
    home = jnp.broadcast_to((mine % NS)[None, :], start.shape)
    total = jnp.broadcast_to(jnp.sum(units, axis=1)[:, None], start.shape)
    figures = jnp.stack([ustart, start, end, home, total], axis=1)
    figures = jnp.pad(figures, ((0, 0), (0, UNIT - USTART - 5), (0, LANES - targets)))
    return jnp.concatenate(
        [order.reshape(blocks, 8, LANES), figures, unit.reshape(blocks, -1, LANES)], axis=1
    )


def product(tiles, table, high, low, targets):
    blocks = table.shape[0]
    inside = pl.BlockSpec(memory_space=pltpu.VMEM)
    return pl.pallas_call(
        product_kernel,
        grid=(blocks,),
        out_shape=jax.ShapeDtypeStruct((targets, HALF, LANES), jnp.float32),
        in_specs=[
            pl.BlockSpec((1,) + table.shape[1:], lambda b: (b, 0, 0), memory_space=pltpu.SMEM),
            inside if blocks == 1 else pl.BlockSpec((BLOCK, HALF, LANES), lambda b: (b, 0, 0)),
            inside,
            inside,
        ],
        out_specs=pl.BlockSpec((targets, HALF, LANES), lambda b: (0, 0, 0)),
        compiler_params=pltpu.CompilerParams(vmem_limit_bytes=SCOPED if blocks == 1 else 44 * 2**20),
    )(table, tiles, high, low)


MESH = pl.DeviceIdType.MESH
PARTS = 6
LINE = 4
CROSS = PARTS - 1


def gather_kernel(
    targets, tiles_ref, ints_ref, ids_ref, all_ref, high_ref, low_ref, table_ref,
    whole_ref, allids_ref, key_ref, packed_ref, units_ref, keys, packeds, positions, unit_counts,
    up_sem, down_sem, over_sem, recv_sem, ids_send, ids_recv, ints_send, ints_recv, local_sem,
):
    pair = lax.axis_index("pair")
    vir = lax.axis_index("vir")
    z, x = pair // 2, pair % 2
    other = pair + 1 - 2 * x
    sibling = vir + 1 - 2 * (vir % 2)
    across = lax.rem(vir + 2, 4)
    depth = ints_ref.shape[0]

    barrier = pltpu.get_barrier_semaphore()
    for k in range(1, 2 * LINE):
        pl.semaphore_signal(
            barrier, inc=1, device_id={"pair": lax.rem(pair + k, 2 * LINE)}, device_id_type=MESH
        )
    for peer in (sibling, across):
        pl.semaphore_signal(barrier, inc=1, device_id={"vir": peer}, device_id_type=MESH)
    pl.semaphore_wait(barrier, 2 * LINE + 1)

    def id_copy(k):
        return pltpu.make_async_remote_copy(
            src_ref=ids_ref, dst_ref=allids_ref.at[pl.ds(pair, 1), :], send_sem=ids_send.at[k - 1],
            recv_sem=ids_recv.at[k - 1], device_id={"pair": lax.rem(pair + k, 2 * LINE)},
            device_id_type=MESH,
        )

    def id_arrival(k):
        source = lax.rem(pair + 2 * LINE - k, 2 * LINE)
        return pltpu.make_async_remote_copy(
            src_ref=ids_ref, dst_ref=allids_ref.at[pl.ds(source, 1), :], send_sem=ids_send.at[k - 1],
            recv_sem=ids_recv.at[k - 1], device_id={"pair": source}, device_id_type=MESH,
        )

    def tile_copy(ref, source, part, sems, peer):
        return pltpu.make_async_remote_copy(
            src_ref=ref, dst_ref=all_ref.at[source, part], send_sem=sems.at[source, part],
            recv_sem=recv_sem.at[source, part], device_id={"pair": peer}, device_id_type=MESH,
        )

    def up(ref, source, part):
        return tile_copy(ref, source, part, up_sem, pair + 2)

    def down(ref, source, part):
        return tile_copy(ref, source, part, down_sem, pair - 2)

    def over(ref, source, part):
        return tile_copy(ref, source, part, over_sem, other)

    def arrive(source, part):
        over(all_ref.at[source, part], source, part).wait_recv()

    def ints_copy(ref, owner, index, peer):
        rows = pl.ds(pl.multiple_of(owner * depth, depth), depth)
        return pltpu.make_async_remote_copy(
            src_ref=ref, dst_ref=whole_ref.at[:, rows, :], send_sem=ints_send.at[index],
            recv_sem=ints_recv.at[index], device_id={"vir": peer}, device_id_type=MESH,
        )

    def rows_of(owner):
        return whole_ref.at[:, pl.ds(pl.multiple_of(owner * depth, depth), depth), :]

    for k in range(1, 2 * LINE):
        id_copy(k).start()

    for part in range(CROSS, PARTS):
        over(tiles_ref.at[part], pair, part).start()

    def own(part, carry):
        @pl.when(z < LINE - 1)
        def _():
            up(tiles_ref.at[part], pair, part).start()

        @pl.when(z > 0)
        def _():
            down(tiles_ref.at[part], pair, part).start()

        @pl.when(part < CROSS)
        def _():
            over(tiles_ref.at[part], pair, part).start()

        return carry

    lax.fori_loop(0, PARTS, own, 0)
    for b in range(NS // 2):
        columns = ints_ref.at[:, pl.ds(b * LANES, LANES)]
        rows = pl.ds(pl.multiple_of(vir * depth, depth), depth)
        pltpu.make_async_copy(columns, whole_ref.at[b, rows, :], local_sem.at[1]).start()
        for index, peer in ((0, across), (1, sibling)):
            pltpu.make_async_remote_copy(
                src_ref=columns, dst_ref=whole_ref.at[b, rows, :], send_sem=ints_send.at[index],
                recv_sem=ints_recv.at[index], device_id={"vir": peer}, device_id_type=MESH,
            ).start()
    locals_ = [
        pltpu.make_async_copy(tiles_ref, all_ref.at[pair], local_sem.at[0]),
        pltpu.make_async_copy(ids_ref, allids_ref.at[pl.ds(pair, 1), :], local_sem.at[2]),
    ]
    for copy in locals_:
        copy.start()
    locals_.pop().wait()
    for k in range(1, 2 * LINE):
        id_arrival(k).wait_recv()

    def to_scalars(source, target):
        copy = pltpu.make_async_copy(source, target, local_sem.at[2])
        copy.start()
        copy.wait()

    def over_tiles(body, initial):
        def device(d, carry):
            return lax.fori_loop(0, targets, lambda i, c: body(d, i, c), carry, unroll=8)

        return lax.fori_loop(0, 2 * LINE, device, initial)

    line = lax.broadcasted_iota(jnp.int32, (8, LANES), 0)
    lane = lax.broadcasted_iota(jnp.int32, (8, LANES), 1)
    slot = line * LANES + lane
    size = 8 * LANES
    ids = allids_ref[...]
    own_key = ids_ref[...] // NS * size
    key = ids // NS * size + slot
    key_ref[...] = key
    packed_ref[...] = (line * targets + lane) * PACK + ids % NS
    to_scalars(key_ref, keys)
    to_scalars(packed_ref, packeds)

    def compare(d, i, carry):
        position, start, end = carry
        value = keys[d, i]
        return (
            position + jnp.where(value < key, 1, 0),
            start + jnp.where(value < own_key, 1, 0),
            end + jnp.where(value < own_key + size, 1, 0),
        )

    zero = jnp.zeros((1, LANES), jnp.int32)
    position, start, end = over_tiles(compare, (jnp.zeros_like(key), zero, zero))
    key_ref[...] = position
    units = (end - start + CHUNK - 1) // CHUNK
    units_ref[...] = units
    to_scalars(key_ref, positions)
    to_scalars(units_ref, unit_counts)

    def place(d, i, order):
        return order + jnp.where(slot == positions[d, i], packeds[d, i], 0)

    table_ref[pl.ds(0, 8), :] = over_tiles(place, jnp.zeros_like(key))
    rows = table_ref.shape[0] - UNIT
    place_of = (
        lax.broadcasted_iota(jnp.int32, (rows, LANES), 0) * LANES
        + lax.broadcasted_iota(jnp.int32, (rows, LANES), 1)
    )

    def count(t, carry):
        total, ustart, unit = carry
        ustart = ustart + jnp.where(lane[:1] > t, unit_counts[0, t], 0)
        total = total + unit_counts[0, t]
        return total, ustart, unit + jnp.where(place_of >= total, 1, 0)

    total, ustart, unit = lax.fori_loop(
        0, targets, count, (jnp.int32(0), zero, jnp.zeros((rows, LANES), jnp.int32))
    )
    table_ref[pl.ds(UNIT, rows), :] = jnp.minimum(unit, targets - 1)
    table_ref[pl.ds(USTART, UNIT - USTART), :] = jnp.concatenate(
        [ustart, start, end, ids_ref[...] % NS, zero + total, zero, zero, zero], axis=0
    )

    def from_below(distance, column, part, crosses):
        source = (z - distance) * 2 + column

        @pl.when(z >= distance)
        def _():
            arrive(source, part)

            @pl.when(z < LINE - 1)
            def _():
                up(all_ref.at[source, part], source, part).start()

            if crosses:
                over(all_ref.at[source, part], source, part).start()

    def from_above(distance, column, part, crosses):
        source = (z + distance) * 2 + column

        @pl.when(z + distance < LINE)
        def _():
            arrive(source, part)

            @pl.when(z > 0)
            def _():
                down(all_ref.at[source, part], source, part).start()

            if crosses:
                over(all_ref.at[source, part], source, part).start()

    for distance in range(1, LINE):

        def step(part, carry, distance=distance):
            from_below(distance, x, part, True)
            from_above(distance, x, part, True)
            return carry

        lax.fori_loop(0, CROSS, step, 0)

        def own_column(part, carry, distance=distance):
            from_below(distance, x, part, False)
            from_above(distance, x, part, False)
            return carry

        def other_column(part, carry, distance=distance):
            if distance > 1:
                from_below(distance - 1, 1 - x, part, False)
                from_above(distance - 1, 1 - x, part, False)
                return carry
            arrive(other, part)

            @pl.when(z < LINE - 1)
            def _():
                up(all_ref.at[other, part], other, part).start()

            @pl.when(z > 0)
            def _():
                down(all_ref.at[other, part], other, part).start()

            return carry

        lax.fori_loop(CROSS, PARTS, own_column, 0)
        lax.fori_loop(CROSS, PARTS, other_column, 0)
        if distance == 2:
            ints_copy(rows_of(across), across, 0, across).wait_recv()
            ints_copy(rows_of(across), across, 2, sibling).start()
    for part in range(CROSS, PARTS):
        from_below(LINE - 1, 1 - x, part, False)
        from_above(LINE - 1, 1 - x, part, False)

    ints_copy(rows_of(sibling), sibling, 1, sibling).wait_recv()
    far = lax.rem(sibling + 2, 4)
    ints_copy(rows_of(far), far, 2, sibling).wait_recv()
    pltpu.make_async_copy(rows_of(vir), rows_of(vir), local_sem.at[1]).wait()

    def split(i, carry):
        rows = pl.ds(pl.multiple_of(i * TS, TS), TS)
        for b in range(NS // 2):
            value = whole_ref[b, rows, :]
            rounded = value.astype(jnp.bfloat16)
            high_ref[b, rows, :] = rounded
            low_ref[b, rows, :] = (value - rounded.astype(jnp.float32)).astype(jnp.bfloat16)
        return carry

    lax.fori_loop(0, NS, split, 0)
    def last(part, carry):
        for k in range(LINE):
            arrive(k * 2 + 1 - x, part)
        return carry

    lax.fori_loop(0, CROSS, last, 0)
    for copy in locals_:
        copy.wait()

    def sent(part, carry):
        for k in range(LINE):
            source = k * 2 + x

            @pl.when((k <= z) & (z < LINE - 1))
            def _():
                up(all_ref.at[source, part], source, part).wait_send()

            @pl.when((k >= z) & (z > 0))
            def _():
                down(all_ref.at[source, part], source, part).wait_send()

            @pl.when((part < CROSS) | (k == z))
            def _():
                over(all_ref.at[source, part], source, part).wait_send()

        return carry

    lax.fori_loop(0, PARTS, sent, 0)

    def crossed(part, carry):
        for k in range(LINE):
            source = k * 2 + 1 - x

            @pl.when((k <= z) & (z < LINE - 1))
            def _():
                up(all_ref.at[source, part], source, part).wait_send()

            @pl.when((k >= z) & (z > 0))
            def _():
                down(all_ref.at[source, part], source, part).wait_send()

        return carry

    lax.fori_loop(CROSS, PARTS, crossed, 0)
    for k in range(1, 2 * LINE):
        id_copy(k).wait_send()
    for index in range(3):
        ints_copy(rows_of(vir), vir, index, sibling).wait_send()


def gathered(tiles, integrals, ids, capacity):
    targets = tiles.shape[0]
    shape = (NS // 2, NS * TS, LANES)
    anywhere = pl.BlockSpec(memory_space=pl.ANY)
    inside = pl.BlockSpec(memory_space=pltpu.VMEM)
    slots = (2 * LINE, PARTS)
    dma = pltpu.SemaphoreType.DMA
    all_tiles, high, low, table = pl.pallas_call(
        functools.partial(gather_kernel, targets),
        out_shape=[
            pltpu.VMEM(slots + (targets // PARTS, HALF, LANES), jnp.float32),
            pltpu.VMEM(shape, jnp.bfloat16),
            pltpu.VMEM(shape, jnp.bfloat16),
            jax.ShapeDtypeStruct((UNIT + unit_rows(targets, capacity), LANES), jnp.int32),
        ],
        in_specs=[anywhere, anywhere, inside],
        out_specs=[inside] * 4,
        scratch_shapes=[pltpu.VMEM(shape, jnp.float32)]
        + [pltpu.VMEM((8, LANES), jnp.int32)] * 3
        + [pltpu.VMEM((1, LANES), jnp.int32)]
        + [pltpu.SMEM((8, LANES), jnp.int32)] * 3
        + [pltpu.SMEM((1, LANES), jnp.int32)]
        + [dma(slots)] * 4 + [dma((2 * LINE - 1,))] * 2 + [dma((3,))] * 3,
        compiler_params=pltpu.CompilerParams(
            collective_id=0, has_side_effects=True, vmem_limit_bytes=SCOPED
        ),
    )(
        tiles.reshape(PARTS, targets // PARTS, HALF, LANES),
        integrals,
        jnp.pad(ids, (0, LANES - targets))[None, :],
    )
    return all_tiles.reshape(-1, HALF, LANES), high, low, table[None]


def per_device(amplitudes, integrals, tile_owner, tile_key):
    targets = amplitudes.shape[0]
    pairs = lax.axis_size("pair")
    mine = tile_owner * (NS * NS) + tile_key
    tiles = amplitudes.reshape(targets, HALF, LANES)
    capacity = max(2, 2 * targets // pairs)
    if pairs == 2 * LINE and lax.axis_size("vir") == 4 and targets * pairs == BLOCK and targets % PARTS == 0:
        tiles, high, low, table = gathered(tiles, integrals, mine, capacity)
    else:
        ids = lax.all_gather(mine, "pair", axis=0, tiled=True)
        whole = lax.all_gather(integrals, "vir", axis=0, tiled=True)
        whole = whole.reshape(-1, NS // 2, LANES).transpose(1, 0, 2)
        tiles = lax.all_gather(tiles, "pair", axis=0, tiled=True)
        rounded = lax.reduce_precision(whole, 8, 7)
        high = rounded.astype(jnp.bfloat16)
        low = (whole - rounded).astype(jnp.bfloat16)
        table = tables(ids, mine, capacity)
    out = product(tiles, table, high, low, targets)
    return out.reshape(targets, TS * TS)


def solution(mesh):
    placed = (P(("pair", "vir"), None), P("vir", None), P(("pair", "vir")), P(("pair", "vir")))
    return jax.shard_map(
        per_device, mesh=mesh, in_specs=placed, out_specs=P(("pair", "vir"), None), check_vma=False
    )
```
